512 devices in a mesh: blk: 256 (over y, z_hi, x, core), rep: 2 (over z_lo).
Axes of the slice: x: 4, y: 8, z: 8 (z_hi: 4, z_lo: 2; z = z_hi * 2 + z_lo), core: 2. Of those that a mesh axis runs over, the one named last changes fastest.
Arguments:
- positions: float32 [3, 262144], P(None, ('blk', 'rep')), may hold values from -5 to 5
- velocities: float32 [3, 262144], P(None, ('blk', 'rep')), may hold values from -5 to 5
- masses: float32 [262144], P(('blk', 'rep')), may hold values from 0.2 to 2
Outputs:
- star_accel: float32 [3, 262144], P(None, ('blk', 'rep'))
- star_jerk: float32 [3, 262144], P(None, ('blk', 'rep'))
The draws below stay inside these ranges and needn't reach their ends.
All inputs are finite; a program needn't handle non-finite values.
Results may differ from the reference program's by a relative error of at most 0.00015.
Values sent between devices are 32-bit elements; how exact they have to be, the bound alone decides.
A program may use at most 64 MiB of HBM per device.

```python
import math
import jax
import jax.numpy as jnp
from jax import lax

BLOCK = 1024
STEPS = 4
STARS = 262144


def level_of(stream_key, shape, cuts, least, high):
    def one(dim, blocks):
        steps = jax.random.uniform(jax.random.fold_in(jax.random.fold_in(stream_key, 6), dim), (blocks,), jnp.float32, least / len(cuts), high / len(cuts))
        return jnp.repeat(jnp.exp(steps), shape[dim] // blocks).reshape((-1,) + (1,) * (len(shape) - dim - 1))

    factor_of = one(*cuts[0])
    for cut in cuts[1:]:
        factor_of = factor_of * one(*cut)
    return factor_of


def centred(own_key, extent, deviation, reach, pieces=(), dtype=jnp.bfloat16):
    values = jax.random.normal(own_key, extent, jnp.float32) * deviation
    if len(pieces) > 0:
        values = level_of(own_key, extent, pieces, -0.22, 0.18) * values
    return jnp.clip(values, min=-reach, max=reach).astype(dtype)


def setup_inputs(seed: int = 0) -> dict:
    splits = jax.random.split(jax.random.key(seed), 4)
    positions = centred(splits[0], (3, STARS), 1.0, 5.0, ((1, 512),), jnp.float32)
    velocities = centred(splits[1], (3, STARS), 1.0, 5.0, ((1, 512),), jnp.float32)
    masses = jnp.clip(jnp.exp(math.log(2.0) - 2.3025851 * jax.random.uniform(splits[2], (STARS,), jnp.float32) ** level_of(splits[2], (STARS,), ((0, 512),), -0.2, 0.2)), 0.2, 2.0)
    return {"positions": positions, "velocities": velocities, "masses": masses}


SOFTENING_SQ = 0.01

def pair_tile(targets, sources):
    coupling = 1.0 / BLOCK
    offset = sources[0:3, None, :] - targets[0:3, :, None]
    closing = sources[3:6, None, :] - targets[3:6, :, None]
    radius_sq = offset[0] * offset[0] + offset[1] * offset[1] + offset[2] * offset[2] + SOFTENING_SQ
    inverse = lax.rsqrt(radius_sq)
    inverse_cube = inverse * inverse * inverse * coupling
    factor = 3.0 * (offset[0] * closing[0] + offset[1] * closing[1] + offset[2] * closing[2]) * inverse * inverse
    pull_term = inverse_cube[None] * offset
    jolt_term = inverse_cube[None] * (closing - factor[None] * offset)
    pair_terms = jnp.concatenate([pull_term, jolt_term], 0)
    own_part = lax.optimization_barrier(jnp.sum(pair_terms * sources[6][None, None, :], 2))
    reaction = -lax.optimization_barrier(jnp.sum(pair_terms * targets[6][None, :, None], 1))
    return (own_part, reaction)

def reference(positions, velocities, masses):
    block_count = positions.shape[1] // BLOCK
    stacked = jnp.concatenate([positions, velocities, masses[None]], 0)
    blocks = stacked.reshape(7, block_count, BLOCK).transpose(1, 0, 2)
    summed = lax.map(lambda single: pair_tile(single, single)[0], blocks)
    for stride in range(1, STEPS + 1):
        partner = jnp.roll(blocks, -stride, 0)
        own_part, reaction = lax.map(lambda pair_in: pair_tile(pair_in[0], pair_in[1]), (blocks, partner))
        summed = summed + own_part + jnp.roll(reaction, stride, 0)
    flattened = summed.transpose(1, 0, 2).reshape(6, block_count * BLOCK)
    return (flattened[0:3], flattened[3:6])
```

```python
import jax
import jax.numpy as jnp
from jax import lax
from jax.experimental import pallas as pl
from jax.experimental.pallas import tpu as pltpu
from jax.sharding import PartitionSpec as P

BLOCK = 1024
STEPS = 4
SOFTENING_SQ = 0.01
PIECES = 3
BF = jnp.bfloat16
F32 = jnp.float32
MESH = pl.DeviceIdType.MESH


def as_bf16(value):
    return value.astype(BF).astype(F32)


def pieces(value, count):
    out = []
    for _ in range(count - 1):
        high = as_bf16(value)
        out.append(high)
        value = value - high
    out.append(as_bf16(value))
    return out


def on_grid(value):
    coarse = jnp.round(value * 32.0) * (1.0 / 32.0)
    rest = value - coarse
    first = as_bf16(rest)
    second = as_bf16(rest - first)
    return coarse, rest, first, second


def added(rows):
    return rows[0:1] + rows[1:2] + rows[2:3]


def products(pos, vel):
    xq, xr, x1, x2 = on_grid(pos)
    vq, vr, v1, v2 = on_grid(vel)
    q = pieces(added(xq * xq), 3)
    s = pieces(added(2.0 * xq * xr + xr * xr), 3)
    dq = pieces(added(xq * vq), 3)
    ds = pieces(added(xq * vr + xr * vq + xr * vr), 3)
    return (xq, x1, x2, vq, v1, v2), (q, s, dq, ds)


def source_rows(pos, vel):
    (xq, x1, x2, vq, v1, v2), (q, s, dq, ds) = products(pos, vel)
    ones = [jnp.ones_like(q[0])] * 3
    square = [xq] + q + ones + [xq, xq, x1, x2, x1, x1, x2] + s + ones
    dot = [xq, vq] + dq + ones + [xq, xq, x1, x2, x1, x1, x2] + [vq, vq, v1, v2, v1, v1, v2] + ds + ones
    return jnp.concatenate(square + dot, 0)


def target_rows(pos, vel):
    (xq, x1, x2, vq, v1, v2), (q, s, dq, ds) = products(pos, vel)
    ones = [jnp.ones_like(q[0])] * 3
    s = pieces(s[0] + s[1] + s[2] + SOFTENING_SQ, 3)
    a, b, c = -2.0 * xq, -2.0 * x1, -2.0 * x2
    square = [a] + ones + q + [b, c, a, a, b, c, b] + ones + s
    dot = [-vq, -xq] + ones + dq + [-v1, -v2, -vq, -vq, -v1, -v2, -v1] + [-x1, -x2, -xq, -xq, -x1, -x2, -x1] + ones + ds
    square = jnp.concatenate(square, 0)
    dot = jnp.concatenate(dot, 0)
    top = jnp.concatenate([square, jnp.zeros_like(square)], 1)
    bottom = jnp.concatenate([jnp.zeros_like(dot), dot], 1)
    return jnp.concatenate([top, bottom], 0)


def value_rows(pos, vel, mass):
    m = mass * (1.0 / BLOCK)
    zero = jnp.zeros_like(m)
    one = pieces(jnp.concatenate([m, m * pos, m * vel, zero], 0), PIECES)
    two = pieces(3.0 * jnp.concatenate([m, m * pos], 0), PIECES) + [jnp.zeros_like(pos[0:1])] * 4
    return jnp.concatenate(one, 0), jnp.concatenate(two, 0)


def kernel(blocks, features, p_ref, v_ref, m_ref, accel_ref, jerk_ref, mine, seen, feat, tgt, val1, val2, sum1, sum2, send_sem, recv_sem):
    blk = lax.axis_index("blk")
    rep = lax.axis_index("rep")
    half = p_ref.shape[1]
    slots = seen.shape[0]

    def offset(k):
        return (k // 2 + 1) * (1 - 2 * (k % 2))

    def peer(k, r):
        return (lax.rem(blk + offset(k) + blocks, blocks), r)

    barrier = pltpu.get_barrier_semaphore()
    pl.semaphore_signal(barrier, inc=1, device_id=(blk, 1 - rep), device_id_type=MESH)
    for k in range(2 * STEPS):
        for r in range(2):
            pl.semaphore_signal(barrier, inc=1, device_id=peer(k, r), device_id_type=MESH)

    mine[0:3] = p_ref[...]
    mine[3:6] = v_ref[...]
    mine[6:7] = m_ref[...]
    mine[7:8] = jnp.zeros((1, half), F32)
    sum1[...] = jnp.zeros_like(sum1)
    sum2[...] = jnp.zeros_like(sum2)

    def prepare(stars, into):
        feat[into] = source_rows(stars[0:3], stars[3:6]).T.astype(BF)
        one, two = value_rows(stars[0:3], stars[3:6], stars[6:7])
        val1[into] = one.astype(BF)
        val2[into] = two.astype(BF)

    def work(at):
        both = jnp.dot(feat[at], tgt[...], preferred_element_type=F32)
        inverse = lax.rsqrt(both[:, :half])
        inverse_sq = inverse * inverse
        w = inverse * inverse_sq
        w2 = w * (both[:, half:] * inverse_sq)
        high = w.astype(BF)
        low = (w - high.astype(F32)).astype(BF)
        high2 = w2.astype(BF)
        low2 = (w2 - high2.astype(F32)).astype(BF)
        one = val1[at]
        two = val2[at]
        sum1[...] += jnp.dot(one, high, preferred_element_type=F32) + jnp.dot(one, low, preferred_element_type=F32)
        sum2[...] += jnp.dot(two, high2, preferred_element_type=F32) + jnp.dot(two, low2, preferred_element_type=F32)

    def copy(src, slot, device, sent):
        return pltpu.make_async_remote_copy(
            src_ref=src,
            dst_ref=seen.at[slot],
            send_sem=send_sem.at[sent],
            recv_sem=recv_sem.at[slot],
            device_id=device,
            device_id_type=MESH,
        )

    own = mine[...]
    tgt[...] = target_rows(own[0:3], own[3:6]).astype(BF)
    prepare(own, 0)

    pl.semaphore_wait(barrier, slots - 1)
    copies = [copy(mine, 1, (blk, 1 - rep), 1)]
    for k in range(2 * STEPS):
        for r in range(2):
            copies.append(copy(mine, 2 + 2 * (k ^ 1) + rep, peer(k, r), 2 + 2 * k + r))
    for one in copies:
        one.start()

    work(0)

    def arrive(slot):
        copy(mine, slot, (blk, 1 - rep), slot).wait_recv()
        prepare(seen[slot], lax.rem(slot, 2))

    arrive(1)

    def step(slot, _):
        arrive(slot + 1)
        work(lax.rem(slot, 2))
        return 0

    lax.fori_loop(1, slots - 1, step, 0)
    work((slots - 1) % 2)

    one = sum1[0:8] + sum1[8:16] + sum1[16:24]
    two = sum2[0:4] + sum2[4:8] + sum2[8:12]
    pos, vel = own[0:3], own[3:6]
    accel_ref[...] = one[1:4] - pos * one[0:1]
    jerk_ref[...] = (one[4:7] - vel * one[0:1]) - (two[1:4] - pos * two[0:1])
    for one in copies:
        one.wait_send()


def body(positions, velocities, masses):
    half = positions.shape[1]
    blocks = lax.axis_size("blk")
    slots = 2 * (2 * STEPS + 1)
    features = 96
    vmem = pl.BlockSpec(memory_space=pltpu.VMEM)
    out = jax.ShapeDtypeStruct((3, half), F32)

    def run(*refs):
        kernel(blocks, features, *refs)

    return pl.pallas_call(
        run,
        out_shape=(out, out),
        in_specs=[vmem] * 3,
        out_specs=(vmem, vmem),
        scratch_shapes=[
            pltpu.VMEM((8, half), F32),
            pltpu.VMEM((slots, 8, half), F32),
            pltpu.VMEM((2, half, features), BF),
            pltpu.VMEM((features, 2 * half), BF),
            pltpu.VMEM((2, 8 * PIECES, half), BF),
            pltpu.VMEM((2, 16, half), BF),
            pltpu.VMEM((8 * PIECES, half), F32),
            pltpu.VMEM((16, half), F32),
            pltpu.SemaphoreType.DMA((slots,)),
            pltpu.SemaphoreType.DMA((slots,)),
        ],
        compiler_params=pltpu.CompilerParams(collective_id=0, has_side_effects=True, vmem_limit_bytes=48 << 20),
    )(positions, velocities, masses[None])


def solution(mesh):
    return jax.shard_map(
        body,
        mesh=mesh,
        in_specs=(P(None, ("blk", "rep")), P(None, ("blk", "rep")), P(("blk", "rep"))),
        out_specs=(P(None, ("blk", "rep")), P(None, ("blk", "rep"))),
        check_vma=False,
    )
```
